32 devices in a mesh: freq: 2 (over x), row: 4 (over y, core), col: 4 (over z).
Axes of the slice: x: 2, y: 2, z: 4, core: 2. Of those that a mesh axis runs over, the one named last changes fastest.
Arguments:
- b_stored: bfloat16 [1536, 6144], P('row', 'col'), may hold values from -0.5 to 0.5
- block_order: int32 [12], replicated, may hold values from 0 to 11, as said below
- pattern: int32 [12, 24], replicated, may hold values from 0 to 1, as said below
- eps_occ: float32 [2], replicated, may hold values from -1 to -0.3
- eps_vir: float32 [3072], replicated, may hold values from 0.1 to 3
- omega: float32 [2], P('freq'), parts along dimension 0, may hold values from 0.2 to 2
Outputs:
- chi_zero: float32 [3072, 1536], P(('freq', 'row'), 'col'), parts along dimension 0
The draws below stay inside these ranges and needn't reach their ends.
There are 2 independent parts, one for each index of `freq`. The reference program is written for one: setup_inputs(seed, part) draws one part's arguments, and reference() takes and returns one part's arrays. A program takes and returns all parts, laid end to end along the dimension named above; an argument that names none is the same for every part. Nothing has to cross between parts.
Inputs may be any that keep to these rules, and one draw needn't show every extreme that they name: `block_order`: each auxiliary block stands in exactly one storage slot. For every pair tile t and every group of storage slots g * 3 to g * 3 + 2, exactly 2 of the blocks block_order[s] held in those slots have pattern 1 at tile t.
All inputs are finite; a program needn't handle non-finite values.
Results may differ from the reference program's by a relative error of at most 0.0013.
Values may be sent and summed in bfloat16 or wider, within the bound.
A program may use at most 64 MiB of HBM per device.

```python
import math
import jax
import jax.numpy as jnp
from jax import lax

BLK = 128
BPR = 3
KEEP = 2
NOCC = 2
NV = 3072
TI = 256
NB = 12
NAUX = 1536
NIA = 6144
NIT = 24


def shared_order(key):
    return jax.random.permutation(key, NB).astype(jnp.int32)


def draw_block_order(key, part):
    return shared_order(key)


def draw_pattern(key, part):
    order = shared_order(key)
    key = jax.random.fold_in(key, 7)
    groups = NB // BPR
    scores = jax.random.randint(key, (groups, BPR, NIT), 0, 1 << 20) * BPR + jnp.arange(BPR, dtype=jnp.int32)[None, :, None]
    ranks = jnp.argsort(jnp.argsort(scores, axis=1), axis=1)
    live = (ranks < KEEP).astype(jnp.int32).reshape(NB, NIT)
    return jnp.zeros((NB, NIT), jnp.int32).at[order].set(live)


def block_levels(own_key, shape, cuts, least, top_value):
    level = 1.0
    for dim, blocks in cuts:
        draws = jax.random.uniform(jax.random.fold_in(jax.random.fold_in(own_key, 6), dim), (blocks,), jnp.float32, least / len(cuts), top_value / len(cuts))
        level = level * jnp.repeat(jnp.exp(draws), shape[dim] // blocks).reshape((-1,) + (1,) * (len(shape) - 1 - dim))
    return level


def bell_draw(key, extent, deviation, bound, cuts=(), held_as=jnp.bfloat16):
    level = block_levels(key, extent, cuts, -0.22, 0.18) if cuts else 1.0
    values = jax.random.normal(key, extent, jnp.float32) * deviation * level
    return jnp.minimum(jnp.maximum(values, -bound), bound).astype(held_as)


def setup_inputs(seed: int = 0, part: int = 0) -> dict:
    arg_keys = jax.random.split(jax.random.key(seed), 7)
    part_splits = jax.random.split(jax.random.fold_in(arg_keys[6], part), 7)
    b_stored = bell_draw(arg_keys[0], (NAUX, NIA), 0.08, 0.5, ((0, 4), (1, 4)))
    block_order = draw_block_order(jax.random.fold_in(arg_keys[6], 71), part)
    pattern = draw_pattern(jax.random.fold_in(arg_keys[6], 71), part)
    eps_occ = jnp.clip(jax.random.uniform(arg_keys[3], (NOCC,), jnp.float32, -1.0, -0.3), -1.0, -0.3)
    eps_vir = jnp.clip(jax.random.uniform(arg_keys[4], (NV,), jnp.float32, 0.1, 3.0), 0.1, 3.0)
    omega = jnp.clip(jnp.exp(jax.random.uniform(part_splits[5], (1,), jnp.float32, math.log(0.2), math.log(2.0))), 0.2, 2.0)
    return {"b_stored": b_stored, "block_order": block_order, "pattern": pattern, "eps_occ": eps_occ, "eps_vir": eps_vir, "omega": omega}


def reference(b_stored, block_order, pattern, eps_occ, eps_vir, omega):
    inverse = jnp.zeros((NB,), jnp.int32).at[block_order].set(jnp.arange(NB, dtype=jnp.int32))
    blocks = b_stored.reshape(NB, BLK, NIA)[inverse]
    screen = jnp.repeat(pattern, TI, axis=1).astype(jnp.float32)
    masked = (blocks.astype(jnp.float32) * screen[:, None, :]).reshape(NAUX, NIA).astype(jnp.bfloat16)
    spacing = (eps_vir[None, :] - eps_occ[:, None]).reshape(NIA)
    weight = 2.0 * spacing / (spacing * spacing + omega[0] * omega[0])
    right = (masked.astype(jnp.float32) * weight[None, :]).astype(jnp.bfloat16)
    return lax.dot_general(masked, right, (((1,), (1,)), ((), ())), preferred_element_type=jnp.float32)
```

```python
import functools
import jax
import jax.numpy as jnp
from jax import lax
from jax.experimental import pallas as pl
from jax.experimental.pallas import tpu as pltpu
from jax.sharding import PartitionSpec as P

BLK = 128
BPR = 3
LIVE = 2
NV = 3072
TI = 256
MESH = pl.DeviceIdType.MESH


def kernel(geo, order, pattern, occ, omega, vir, b_hbm, out, *scratch):
    rows, cols, chunks, tiles = geo
    wide = tiles * TI
    pairs = chunks * wide
    blocks = rows * BPR
    chips = rows // 2
    own_cols = blocks * BLK // cols
    stage, gath = scratch[:chunks], scratch[chunks : 2 * chunks]
    (inv, weight, left, right, sent, landed, in_sem, core_s, core_r, y_s, y_r, x_s, x_r,
     yc_s, yc_r, xc_s, xc_r, z_s, z_r) = scratch[2 * chunks :]
    x, r, z = lax.axis_index("freq"), lax.axis_index("row"), lax.axis_index("col")
    y = r // 2
    core = r - 2 * y
    mate = 2 * y + 1 - core

    loads = [
        pltpu.make_async_copy(b_hbm.at[:, :, pl.ds(j * wide, wide)], stage[j], in_sem.at[j])
        for j in range(chunks)
    ]
    for load in loads:
        load.start()

    barrier = pltpu.get_barrier_semaphore()

    def greet(where):
        pl.semaphore_signal(barrier, inc=1, device_id=where, device_id_type=MESH)

    greet({"row": mate})
    greet({"freq": 1 - x})
    for m in range(1, chips):
        greet({"row": 2 * lax.rem(y + m, chips) + core})
    for m in range(1, cols):
        greet({"col": z ^ m})

    def far(m, back):
        return 2 * lax.rem(y + (chips - m if back else m), chips) + core

    def remote(ref, send, recv, where):
        return pltpu.make_async_remote_copy(
            src_ref=ref, dst_ref=ref, send_sem=send, recv_sem=recv, device_id=where, device_id_type=MESH
        )

    def to_core(j, g):
        return remote(gath[j].at[pl.ds(LIVE * g, LIVE)], core_s.at[j], core_r.at[j], {"row": mate})

    def to_y(j, m, g, where):
        return remote(gath[j].at[LIVE * g + x], y_s.at[j, m - 1], y_r.at[j, m - 1], {"row": where})

    def to_x(j, m, g, half):
        return remote(gath[j].at[LIVE * g + half], x_s.at[j, m - 1], x_r.at[j, m - 1], {"freq": 1 - x})

    def y_core(j, m, g):
        return remote(gath[j].at[LIVE * g + x], yc_s.at[j, m - 1], yc_r.at[j, m - 1], {"row": mate})

    def x_core(j, m, g):
        return remote(gath[j].at[LIVE * g + 1 - x], xc_s.at[j, m - 1], xc_r.at[j, m - 1], {"row": mate})

    first_tile = z * (chunks * tiles)
    for j in range(chunks):
        loads[j].wait()
        for t in range(tiles):
            tile = first_tile + j * tiles + t
            span = pl.ds(t * TI, TI)
            low = pattern[order[BPR * r], tile]
            high = pattern[order[BPR * r + 2], tile]
            gath[j][LIVE * r, :, span] = stage[j][1 - low, :, span]
            gath[j][LIVE * r + 1, :, span] = stage[j][1 + high, :, span]
        if j == 0:
            pl.semaphore_wait(barrier, 2 + (chips - 1) + (cols - 1))
        for m in range(1, chips):
            to_y(j, m, r, far(m, False)).start()
        to_core(j, r).start()

    @pl.loop(0, blocks)
    def _(q):
        slot = jnp.int32(0)
        for s in range(blocks):
            slot = jnp.where(order[s] == q, s, slot)
        inv[q] = slot

    offset = z * pairs
    occ_index = offset // NV
    vir_first = pl.multiple_of(offset - occ_index * NV, TI)
    spacing = vir[:, pl.ds(vir_first, pairs)] - occ[occ_index]
    weight[...] = 2.0 * spacing / (spacing * spacing + omega[0] * omega[0])

    for j in range(chunks):
        for m in range(1, chips):
            g = far(m, True)
            to_y(j, m, g, r ^ 1).wait_recv()
            to_x(j, m, g, x).start()
            y_core(j, m, g).start()

    for j in range(chunks):
        for m in range(1, chips):
            g = far(m, True)
            to_x(j, m, g, 1 - x).wait_recv()
            x_core(j, m, g).start()
        to_core(j, mate).wait_recv()
        for m in range(1, chips):
            g = 2 * (far(m, True) // 2) + 1 - core
            y_core(j, m, g).wait_recv()
            x_core(j, m, g).wait_recv()

        def place(q, t):
            tile = first_tile + j * tiles + t
            slot = inv[q]
            group = slot // BPR
            at = slot - BPR * group
            low = pattern[order[BPR * group], tile]
            k = jnp.where(at == 2, 1, jnp.where(at == 1, low, 0))
            return gath[j][LIVE * group + k, :, t * TI : (t + 1) * TI], pattern[q, tile].astype(jnp.float32)

        @pl.loop(0, blocks)
        def _(q):
            for t in range(tiles):
                span = pl.ds(j * wide + t * TI, TI)
                value, live = place(q, t)
                right[pl.ds(pl.multiple_of(q * BLK, BLK), BLK), span] = (
                    value.astype(jnp.float32) * (weight[:, span] * live)
                ).astype(jnp.bfloat16)

        @pl.loop(0, BPR)
        def _(i):
            for t in range(tiles):
                span = pl.ds(j * wide + t * TI, TI)
                value, live = place(BPR * r + i, t)
                left[pl.ds(pl.multiple_of(i * BLK, BLK), BLK), span] = (
                    value.astype(jnp.float32) * live
                ).astype(jnp.bfloat16)

    def share(c):
        return lax.dot_general(
            left[...],
            right[pl.ds(pl.multiple_of(c * own_cols, BLK), own_cols), :],
            (((1,), (1,)), ((), ())),
            preferred_element_type=jnp.float32,
        )

    def to_z(m):
        return pltpu.make_async_remote_copy(
            src_ref=sent.at[m - 1], dst_ref=landed.at[m - 1], send_sem=z_s.at[m - 1], recv_sem=z_r.at[m - 1],
            device_id={"col": z ^ m}, device_id_type=MESH,
        )

    for m in range(cols - 1, 0, -1):
        sent[m - 1] = share(z ^ m).astype(jnp.bfloat16)
        to_z(m).start()
    out[...] = share(z)
    for m in range(cols - 1, 0, -1):
        to_z(m).wait_recv()
        out[...] += landed[m - 1].astype(jnp.float32)

    for m in range(1, cols):
        to_z(m).wait_send()
    for j in range(chunks):
        to_core(j, r).wait_send()
        for m in range(1, chips):
            g = far(m, True)
            to_y(j, m, r, far(m, False)).wait_send()
            to_x(j, m, g, x).wait_send()
            y_core(j, m, g).wait_send()
            x_core(j, m, g).wait_send()


def shards(rows, cols, b_stored, block_order, pattern, eps_occ, eps_vir, omega):
    pairs = b_stored.shape[1]
    count = pairs // TI
    tiles = 2 if count % 2 == 0 else 1
    chunks = count // tiles
    wide = tiles * TI
    chips = rows // 2
    height = b_stored.shape[0]
    own_cols = rows * height // cols
    dma = pltpu.SemaphoreType.DMA
    hop = dma((chunks, max(chips - 1, 1)))
    smem = pl.BlockSpec(memory_space=pltpu.SMEM)
    vmem = pl.BlockSpec(memory_space=pltpu.VMEM)
    return pl.pallas_call(
        functools.partial(kernel, (rows, cols, chunks, tiles)),
        out_shape=jax.ShapeDtypeStruct((height, own_cols), jnp.float32),
        in_specs=[smem, smem, smem, smem, vmem, pl.BlockSpec(memory_space=pl.ANY)],
        out_specs=vmem,
        scratch_shapes=[pltpu.VMEM((BPR, BLK, wide), jnp.bfloat16) for _ in range(chunks)]
        + [pltpu.VMEM((LIVE * rows, BLK, wide), jnp.bfloat16) for _ in range(chunks)]
        + [
            pltpu.SMEM((rows * BPR,), jnp.int32),
            pltpu.VMEM((1, pairs), jnp.float32),
            pltpu.VMEM((height, pairs), jnp.bfloat16),
            pltpu.VMEM((rows * height, pairs), jnp.bfloat16),
            pltpu.VMEM((cols - 1, height, own_cols), jnp.bfloat16),
            pltpu.VMEM((cols - 1, height, own_cols), jnp.bfloat16),
            dma((chunks,)),
            dma((chunks,)),
            dma((chunks,)),
            hop, hop, hop, hop, hop, hop, hop, hop,
            dma((cols - 1,)),
            dma((cols - 1,)),
        ],
        compiler_params=pltpu.CompilerParams(
            collective_id=0, has_side_effects=True, vmem_limit_bytes=56 * 2**20
        ),
        cost_estimate=pl.CostEstimate(
            flops=2 * height * rows * height * pairs, bytes_accessed=4 * height * pairs, transcendentals=0
        ),
    )(block_order, pattern, eps_occ, omega, eps_vir.reshape(1, -1), b_stored.reshape(BPR, BLK, pairs))


def solution(mesh):
    placed = (P("row", "col"), P(), P(), P(), P(), P("freq"))
    return jax.shard_map(
        functools.partial(shards, mesh.shape["row"], mesh.shape["col"]),
        mesh=mesh,
        in_specs=placed,
        out_specs=P(("freq", "row"), "col"),
        check_vma=False,
    )
```

```python
import functools
import jax
import jax.numpy as jnp
from jax import lax
from jax.experimental import pallas as pl
from jax.experimental.pallas import tpu as pltpu
from jax.sharding import PartitionSpec as P

BLK = 128
BPR = 3
LIVE = 2
NV = 3072
TI = 256
MESH = pl.DeviceIdType.MESH


def kernel(geo, order, pattern, occ, omega, vir, b_hbm, out, *scratch):
    rows, cols, chunks, tiles = geo
    wide = tiles * TI
    pairs = chunks * wide
    blocks = rows * BPR
    chips = rows // 2
    own_cols = blocks * BLK // cols
    stage, gath = scratch[:chunks], scratch[chunks : 2 * chunks]
    (inv, weight, left, right, sent, landed, in_sem, core_s, core_r, y_s, y_r, x_s, x_r,
     yc_s, yc_r, xc_s, xc_r, z_s, z_r) = scratch[2 * chunks :]
    x, r, z = lax.axis_index("freq"), lax.axis_index("row"), lax.axis_index("col")
    y = r // 2
    core = r - 2 * y
    mate = 2 * y + 1 - core

    loads = [
        pltpu.make_async_copy(b_hbm.at[:, :, pl.ds(j * wide, wide)], stage[j], in_sem.at[j])
        for j in range(chunks)
    ]
    for load in loads:
        load.start()

    barrier = pltpu.get_barrier_semaphore()

    def greet(where):
        pl.semaphore_signal(barrier, inc=1, device_id=where, device_id_type=MESH)

    greet({"row": mate})
    greet({"freq": 1 - x})
    for m in range(1, chips):
        greet({"row": 2 * lax.rem(y + m, chips) + core})
    for m in range(1, cols):
        greet({"col": z ^ m})

    def far(m, back):
        return 2 * lax.rem(y + (chips - m if back else m), chips) + core

    def remote(ref, send, recv, where):
        return pltpu.make_async_remote_copy(
            src_ref=ref, dst_ref=ref, send_sem=send, recv_sem=recv, device_id=where, device_id_type=MESH
        )

    def to_core(j, g):
        return remote(gath[j].at[pl.ds(LIVE * g, LIVE)], core_s.at[j], core_r.at[j], {"row": mate})

    def to_y(j, m, g, where):
        return remote(gath[j].at[LIVE * g + x], y_s.at[j, m - 1], y_r.at[j, m - 1], {"row": where})

    def to_x(j, m, g, half):
        return remote(gath[j].at[LIVE * g + half], x_s.at[j, m - 1], x_r.at[j, m - 1], {"freq": 1 - x})

    def y_core(j, m, g):
        return remote(gath[j].at[LIVE * g + x], yc_s.at[j, m - 1], yc_r.at[j, m - 1], {"row": mate})

    def x_core(j, m, g):
        return remote(gath[j].at[LIVE * g + 1 - x], xc_s.at[j, m - 1], xc_r.at[j, m - 1], {"row": mate})

    first_tile = z * (chunks * tiles)
    for j in range(chunks):
        loads[j].wait()
        for t in range(tiles):
            tile = first_tile + j * tiles + t
            span = pl.ds(t * TI, TI)
            low = pattern[order[BPR * r], tile]
            high = pattern[order[BPR * r + 2], tile]
            gath[j][LIVE * r, :, span] = stage[j][1 - low, :, span]
            gath[j][LIVE * r + 1, :, span] = stage[j][1 + high, :, span]
        if j == 0:
            pl.semaphore_wait(barrier, 2 + (chips - 1) + (cols - 1))
        for m in range(1, chips):
            to_y(j, m, r, far(m, False)).start()
        to_core(j, r).start()

    @pl.loop(0, blocks)
    def _(q):
        slot = jnp.int32(0)
        for s in range(blocks):
            slot = jnp.where(order[s] == q, s, slot)
        inv[q] = slot

    offset = z * pairs
    occ_index = offset // NV
    vir_first = pl.multiple_of(offset - occ_index * NV, TI)
    spacing = vir[:, pl.ds(vir_first, pairs)] - occ[occ_index]
    weight[...] = 2.0 * spacing / (spacing * spacing + omega[0] * omega[0])

    for j in range(chunks):
        for m in range(1, chips):
            g = far(m, True)
            to_y(j, m, g, r ^ 1).wait_recv()
            to_x(j, m, g, x).start()
            y_core(j, m, g).start()

    for j in range(chunks):
        for m in range(1, chips):
            g = far(m, True)
            to_x(j, m, g, 1 - x).wait_recv()
            x_core(j, m, g).start()
        to_core(j, mate).wait_recv()
        for m in range(1, chips):
            g = 2 * (far(m, True) // 2) + 1 - core
            y_core(j, m, g).wait_recv()
            x_core(j, m, g).wait_recv()

        def place(q, t):
            tile = first_tile + j * tiles + t
            slot = inv[q]
            group = slot // BPR
            at = slot - BPR * group
            low = pattern[order[BPR * group], tile]
            k = jnp.where(at == 2, 1, jnp.where(at == 1, low, 0))
            return gath[j][LIVE * group + k, :, t * TI : (t + 1) * TI], pattern[q, tile].astype(jnp.float32)

        @pl.loop(0, blocks)
        def _(q):
            for t in range(tiles):
                span = pl.ds(j * wide + t * TI, TI)
                value, live = place(q, t)
                right[pl.ds(pl.multiple_of(q * BLK, BLK), BLK), span] = (
                    value.astype(jnp.float32) * (weight[:, span] * live)
                ).astype(jnp.bfloat16)

        @pl.loop(0, BPR)
        def _(i):
            for t in range(tiles):
                span = pl.ds(j * wide + t * TI, TI)
                value, live = place(BPR * r + i, t)
                left[pl.ds(pl.multiple_of(i * BLK, BLK), BLK), span] = (
                    value.astype(jnp.float32) * live
                ).astype(jnp.bfloat16)

    def share(c):
        return lax.dot_general(
            left[...],
            right[pl.ds(pl.multiple_of(c * own_cols, BLK), own_cols), :],
            (((1,), (1,)), ((), ())),
            preferred_element_type=jnp.float32,
        )

    def to_z(m):
        return pltpu.make_async_remote_copy(
            src_ref=sent.at[m - 1], dst_ref=landed.at[m - 1], send_sem=z_s.at[m - 1], recv_sem=z_r.at[m - 1],
            device_id={"col": z ^ m}, device_id_type=MESH,
        )

    for m in range(cols - 1, 0, -1):
        sent[m - 1] = share(z ^ m).astype(jnp.bfloat16)
        to_z(m).start()
    out[...] = share(z)
    for m in range(cols - 1, 0, -1):
        to_z(m).wait_recv()
        out[...] += landed[m - 1].astype(jnp.float32)

    for m in range(1, cols):
        to_z(m).wait_send()
    for j in range(chunks):
        to_core(j, r).wait_send()
        for m in range(1, chips):
            g = far(m, True)
            to_y(j, m, r, far(m, False)).wait_send()
            to_x(j, m, g, x).wait_send()
            y_core(j, m, g).wait_send()
            x_core(j, m, g).wait_send()


def shards(rows, cols, b_stored, block_order, pattern, eps_occ, eps_vir, omega):
    pairs = b_stored.shape[1]
    count = pairs // TI
    tiles = 1
    chunks = count // tiles
    wide = tiles * TI
    chips = rows // 2
    height = b_stored.shape[0]
    own_cols = rows * height // cols
    dma = pltpu.SemaphoreType.DMA
    hop = dma((chunks, max(chips - 1, 1)))
    smem = pl.BlockSpec(memory_space=pltpu.SMEM)
    vmem = pl.BlockSpec(memory_space=pltpu.VMEM)
    return pl.pallas_call(
        functools.partial(kernel, (rows, cols, chunks, tiles)),
        out_shape=jax.ShapeDtypeStruct((height, own_cols), jnp.float32),
        in_specs=[smem, smem, smem, smem, vmem, pl.BlockSpec(memory_space=pl.ANY)],
        out_specs=vmem,
        scratch_shapes=[pltpu.VMEM((BPR, BLK, wide), jnp.bfloat16) for _ in range(chunks)]
        + [pltpu.VMEM((LIVE * rows, BLK, wide), jnp.bfloat16) for _ in range(chunks)]
        + [
            pltpu.SMEM((rows * BPR,), jnp.int32),
            pltpu.VMEM((1, pairs), jnp.float32),
            pltpu.VMEM((height, pairs), jnp.bfloat16),
            pltpu.VMEM((rows * height, pairs), jnp.bfloat16),
            pltpu.VMEM((cols - 1, height, own_cols), jnp.bfloat16),
            pltpu.VMEM((cols - 1, height, own_cols), jnp.bfloat16),
            dma((chunks,)),
            dma((chunks,)),
            dma((chunks,)),
            hop, hop, hop, hop, hop, hop, hop, hop,
            dma((cols - 1,)),
            dma((cols - 1,)),
        ],
        compiler_params=pltpu.CompilerParams(
            collective_id=0, has_side_effects=True, vmem_limit_bytes=56 * 2**20
        ),
        cost_estimate=pl.CostEstimate(
            flops=2 * height * rows * height * pairs, bytes_accessed=4 * height * pairs, transcendentals=0
        ),
    )(block_order, pattern, eps_occ, omega, eps_vir.reshape(1, -1), b_stored.reshape(BPR, BLK, pairs))


def solution(mesh):
    placed = (P("row", "col"), P(), P(), P(), P(), P("freq"))
    return jax.shard_map(
        functools.partial(shards, mesh.shape["row"], mesh.shape["col"]),
        mesh=mesh,
        in_specs=placed,
        out_specs=P(("freq", "row"), "col"),
        check_vma=False,
    )
```

```python
import functools
import jax
import jax.numpy as jnp
from jax import lax
from jax.experimental import pallas as pl
from jax.experimental.pallas import tpu as pltpu
from jax.sharding import PartitionSpec as P

BLK = 128
BPR = 3
LIVE = 2
NV = 3072
EXTRA = 16
TI = 256
MESH = pl.DeviceIdType.MESH


def kernel(geo, order, pattern, occ, omega, vir, b_hbm, out, *scratch):
    rows, cols, chunks, tiles = geo
    wide = tiles * TI
    pairs = chunks * wide
    blocks = rows * BPR
    chips = rows // 2
    own_cols = blocks * BLK // cols
    height = BPR * BLK
    stage, gath = scratch[:chunks], scratch[chunks : 2 * chunks]
    (inv, weight, left, right, sent, landed, relay, in_sem, core_s, core_r, y_s, y_r, x_s, x_r,
     yc_s, yc_r, xc_s, xc_r, z_s, z_r, relay_r) = scratch[2 * chunks :]
    x, r, z = lax.axis_index("freq"), lax.axis_index("row"), lax.axis_index("col")
    y = r // 2
    core = r - 2 * y
    mate = 2 * y + 1 - core

    loads = [
        pltpu.make_async_copy(b_hbm.at[:, :, pl.ds(j * wide, wide)], stage[j], in_sem.at[j])
        for j in range(chunks)
    ]
    for load in loads:
        load.start()

    barrier = pltpu.get_barrier_semaphore()

    def greet(where):
        pl.semaphore_signal(barrier, inc=1, device_id=where, device_id_type=MESH)

    greet({"row": mate})
    greet({"freq": 1 - x})
    for m in range(1, chips):
        greet({"row": 2 * lax.rem(y + m, chips) + core})
    for m in range(1, cols):
        greet({"col": z ^ m})

    def far(m, back):
        return 2 * lax.rem(y + (chips - m if back else m), chips) + core

    def remote(ref, send, recv, where):
        return pltpu.make_async_remote_copy(
            src_ref=ref, dst_ref=ref, send_sem=send, recv_sem=recv, device_id=where, device_id_type=MESH
        )

    def to_core(j, g):
        return remote(gath[j].at[pl.ds(LIVE * g, LIVE)], core_s.at[j], core_r.at[j], {"row": mate})

    def to_y(j, m, g, where):
        return remote(gath[j].at[LIVE * g + x], y_s.at[j, m - 1], y_r.at[j, m - 1], {"row": where})

    def to_x(j, m, g, half):
        return remote(gath[j].at[LIVE * g + half], x_s.at[j, m - 1], x_r.at[j, m - 1], {"freq": 1 - x})

    def y_core(j, m, g):
        return remote(gath[j].at[LIVE * g + x], yc_s.at[j, m - 1], yc_r.at[j, m - 1], {"row": mate})

    def x_core(j, m, g):
        return remote(gath[j].at[LIVE * g + 1 - x], xc_s.at[j, m - 1], xc_r.at[j, m - 1], {"row": mate})

    first_tile = z * (chunks * tiles)
    for j in range(chunks):
        loads[j].wait()
        for t in range(tiles):
            tile = first_tile + j * tiles + t
            span = pl.ds(t * TI, TI)
            low = pattern[order[BPR * r], tile]
            high = pattern[order[BPR * r + 2], tile]
            gath[j][LIVE * r, :, span] = stage[j][1 - low, :, span]
            gath[j][LIVE * r + 1, :, span] = stage[j][1 + high, :, span]
        if j == 0:
            pl.semaphore_wait(barrier, 2 + (chips - 1) + (cols - 1))
        for m in range(1, chips):
            to_y(j, m, r, far(m, False)).start()
        to_core(j, r).start()

    @pl.loop(0, blocks)
    def _(q):
        slot = jnp.int32(0)
        for s in range(blocks):
            slot = jnp.where(order[s] == q, s, slot)
        inv[q] = slot

    offset = z * pairs
    occ_index = offset // NV
    vir_first = pl.multiple_of(offset - occ_index * NV, TI)
    spacing = vir[:, pl.ds(vir_first, pairs)] - occ[occ_index]
    weight[...] = 2.0 * spacing / (spacing * spacing + omega[0] * omega[0])

    for j in range(chunks):
        for m in range(1, chips):
            g = far(m, True)
            to_y(j, m, g, r ^ 1).wait_recv()
            to_x(j, m, g, x).start()
            y_core(j, m, g).start()

    for j in range(chunks):
        for m in range(1, chips):
            g = far(m, True)
            to_x(j, m, g, 1 - x).wait_recv()
            x_core(j, m, g).start()
        to_core(j, mate).wait_recv()
        for m in range(1, chips):
            g = 2 * (far(m, True) // 2) + 1 - core
            y_core(j, m, g).wait_recv()
            x_core(j, m, g).wait_recv()

        def place(q, t):
            tile = first_tile + j * tiles + t
            slot = inv[q]
            group = slot // BPR
            at = slot - BPR * group
            low = pattern[order[BPR * group], tile]
            k = jnp.where(at == 2, 1, jnp.where(at == 1, low, 0))
            return gath[j][LIVE * group + k, :, t * TI : (t + 1) * TI], pattern[q, tile].astype(jnp.float32)

        @pl.loop(0, blocks)
        def _(q):
            for t in range(tiles):
                span = pl.ds(j * wide + t * TI, TI)
                value, live = place(q, t)
                right[pl.ds(pl.multiple_of(q * BLK, BLK), BLK), span] = (
                    value.astype(jnp.float32) * (weight[:, span] * live)
                ).astype(jnp.bfloat16)

        @pl.loop(0, BPR)
        def _(i):
            for t in range(tiles):
                span = pl.ds(j * wide + t * TI, TI)
                value, live = place(BPR * r + i, t)
                left[pl.ds(pl.multiple_of(i * BLK, BLK), BLK), span] = (
                    value.astype(jnp.float32) * live
                ).astype(jnp.bfloat16)

    def share(c):
        return lax.dot_general(
            left[...],
            right[pl.ds(pl.multiple_of(c * own_cols, BLK), own_cols), :],
            (((1,), (1,)), ((), ())),
            preferred_element_type=jnp.float32,
        )

    pair = z // 2
    odd = lax.rem(pair, 2)
    inner = 2 * pair + 1 - odd
    outer = 2 * pair + odd
    relays = cols - 2

    def target(i):
        other = pair ^ (1 + i // 2)
        return 2 * other + (lax.rem(other, 2) if i % 2 == 0 else 1 - lax.rem(other, 2))

    def to_mate():
        return pltpu.make_async_remote_copy(
            src_ref=sent.at[relays], dst_ref=landed.at[0], send_sem=z_s.at[relays], recv_sem=z_r.at[0],
            device_id={"col": z ^ 1}, device_id_type=MESH,
        )

    def to_relay(i):
        return pltpu.make_async_remote_copy(
            src_ref=sent.at[i], dst_ref=relay.at[i], send_sem=z_s.at[i], recv_sem=relay_r.at[i],
            device_id={"col": z ^ 1}, device_id_type=MESH,
        )

    def to_target(i):
        m = 1 + i // 2
        return pltpu.make_async_remote_copy(
            src_ref=sent.at[i], dst_ref=landed.at[m], send_sem=z_s.at[i], recv_sem=z_r.at[m],
            device_id={"col": target(i)}, device_id_type=MESH,
        )

    gap = lax.broadcasted_iota(jnp.int32, (height, own_cols), 1) - lax.broadcasted_iota(
        jnp.int32, (height, own_cols), 0
    )

    def pack(i, value, c):
        rounded = value.astype(jnp.bfloat16)
        sent[i, pl.ds(0, height), :] = rounded
        rest = jnp.where(gap == r * height - c * own_cols, value - rounded.astype(jnp.float32), 0.0)
        sent[i, pl.ds(height, EXTRA), :] = jnp.broadcast_to(
            jnp.sum(rest, axis=0, keepdims=True), (EXTRA, own_cols)
        ).astype(jnp.bfloat16)

    def unpack(ref, i, c):
        rest = ref[i, pl.ds(height, EXTRA), :].astype(jnp.float32)[0:1]
        return ref[i, pl.ds(0, height), :].astype(jnp.float32) + jnp.where(
            gap == r * height - c * own_cols, rest, 0.0
        )

    @pl.when(z == outer)
    def _():
        for i in range(relays):
            pack(i, share(target(i)), target(i))
            to_relay(i).start()
        pack(relays, share(inner), inner)
        to_mate().start()

    @pl.when(z == inner)
    def _():
        pack(relays, share(outer), outer)
        to_mate().start()
        for i in range(relays):
            out[...] = share(target(i))
            to_relay(i).wait_recv()
            pack(i, out[...] + unpack(relay, i, target(i)), target(i))
            to_target(i).start()

    out[...] = share(z)
    for m in range(cols // 2):
        (to_mate() if m == 0 else to_target(2 * (m - 1))).wait_recv()
        out[...] += unpack(landed, m, z)
    to_mate().wait_send()
    for i in range(relays):
        to_relay(i).wait_send()
    for j in range(chunks):
        to_core(j, r).wait_send()
        for m in range(1, chips):
            g = far(m, True)
            to_y(j, m, r, far(m, False)).wait_send()
            to_x(j, m, g, x).wait_send()
            y_core(j, m, g).wait_send()
            x_core(j, m, g).wait_send()


def shards(rows, cols, b_stored, block_order, pattern, eps_occ, eps_vir, omega):
    pairs = b_stored.shape[1]
    count = pairs // TI
    tiles = 2 if count % 2 == 0 else 1
    chunks = count // tiles
    wide = tiles * TI
    chips = rows // 2
    height = b_stored.shape[0]
    own_cols = rows * height // cols
    dma = pltpu.SemaphoreType.DMA
    hop = dma((chunks, max(chips - 1, 1)))
    smem = pl.BlockSpec(memory_space=pltpu.SMEM)
    vmem = pl.BlockSpec(memory_space=pltpu.VMEM)
    return pl.pallas_call(
        functools.partial(kernel, (rows, cols, chunks, tiles)),
        out_shape=jax.ShapeDtypeStruct((height, own_cols), jnp.float32),
        in_specs=[smem, smem, smem, smem, vmem, pl.BlockSpec(memory_space=pl.ANY)],
        out_specs=vmem,
        scratch_shapes=[pltpu.VMEM((BPR, BLK, wide), jnp.bfloat16) for _ in range(chunks)]
        + [pltpu.VMEM((LIVE * rows, BLK, wide), jnp.bfloat16) for _ in range(chunks)]
        + [
            pltpu.SMEM((rows * BPR,), jnp.int32),
            pltpu.VMEM((1, pairs), jnp.float32),
            pltpu.VMEM((height, pairs), jnp.bfloat16),
            pltpu.VMEM((rows * height, pairs), jnp.bfloat16),
            pltpu.VMEM((cols - 1, height + EXTRA, own_cols), jnp.bfloat16),
            pltpu.VMEM((cols // 2, height + EXTRA, own_cols), jnp.bfloat16),
            pltpu.VMEM((cols - 2, height + EXTRA, own_cols), jnp.bfloat16),
            dma((chunks,)),
            dma((chunks,)),
            dma((chunks,)),
            hop, hop, hop, hop, hop, hop, hop, hop,
            dma((cols - 1,)),
            dma((cols // 2,)),
            dma((cols - 2,)),
        ],
        compiler_params=pltpu.CompilerParams(
            collective_id=0, has_side_effects=True, vmem_limit_bytes=56 * 2**20
        ),
        cost_estimate=pl.CostEstimate(
            flops=2 * height * rows * height * pairs, bytes_accessed=4 * height * pairs, transcendentals=0
        ),
    )(block_order, pattern, eps_occ, omega, eps_vir.reshape(1, -1), b_stored.reshape(BPR, BLK, pairs))


def solution(mesh):
    placed = (P("row", "col"), P(), P(), P(), P(), P("freq"))
    return jax.shard_map(
        functools.partial(shards, mesh.shape["row"], mesh.shape["col"]),
        mesh=mesh,
        in_specs=placed,
        out_specs=P(("freq", "row"), "col"),
        check_vma=False,
    )
```

```python
import functools
import jax
import jax.numpy as jnp
from jax import lax
from jax.experimental import pallas as pl
from jax.experimental.pallas import tpu as pltpu
from jax.sharding import PartitionSpec as P

BLK = 128
BPR = 3
LIVE = 2
NV = 3072
EXTRA = 16
TI = 256
MESH = pl.DeviceIdType.MESH


def kernel(geo, order, pattern, occ, omega, vir, b_hbm, out, *scratch):
    rows, cols, chunks, tiles = geo
    wide = tiles * TI
    pairs = chunks * wide
    blocks = rows * BPR
    chips = rows // 2
    own_cols = blocks * BLK // cols
    height = BPR * BLK
    stage, gath = scratch[:chunks], scratch[chunks : 2 * chunks]
    (inv, weight, left, right, sent, landed, relay, in_sem, core_s, core_r, y_s, y_r, x_s, x_r,
     yc_s, yc_r, xc_s, xc_r, z_s, z_r, relay_r) = scratch[2 * chunks :]
    x, r, z = lax.axis_index("freq"), lax.axis_index("row"), lax.axis_index("col")
    y = r // 2
    core = r - 2 * y
    mate = 2 * y + 1 - core

    loads = [
        pltpu.make_async_copy(b_hbm.at[:, :, pl.ds(j * wide, wide)], stage[j], in_sem.at[j])
        for j in range(chunks)
    ]
    for load in loads:
        load.start()

    barrier = pltpu.get_barrier_semaphore()

    def greet(where):
        pl.semaphore_signal(barrier, inc=1, device_id=where, device_id_type=MESH)

    greet({"row": mate})
    greet({"freq": 1 - x})
    for m in range(1, chips):
        greet({"row": 2 * lax.rem(y + m, chips) + core})
    for m in range(1, cols):
        greet({"col": z ^ m})

    def far(m, back):
        return 2 * lax.rem(y + (chips - m if back else m), chips) + core

    def remote(ref, send, recv, where):
        return pltpu.make_async_remote_copy(
            src_ref=ref, dst_ref=ref, send_sem=send, recv_sem=recv, device_id=where, device_id_type=MESH
        )

    def part(j, g):
        return gath[j].at[pl.ds(LIVE * g, LIVE)] if j == chunks - 1 else gath[j].at[LIVE * g + x]

    def to_core(j, g):
        return remote(gath[j].at[pl.ds(LIVE * g, LIVE)], core_s.at[j], core_r.at[j], {"row": mate})

    def to_y(j, m, g, where):
        return remote(part(j, g), y_s.at[j, m - 1], y_r.at[j, m - 1], {"row": where})

    def to_x(j, m, g, half):
        return remote(gath[j].at[LIVE * g + half], x_s.at[j, m - 1], x_r.at[j, m - 1], {"freq": 1 - x})

    def y_core(j, m, g):
        return remote(part(j, g), yc_s.at[j, m - 1], yc_r.at[j, m - 1], {"row": mate})

    def x_core(j, m, g):
        return remote(gath[j].at[LIVE * g + 1 - x], xc_s.at[j, m - 1], xc_r.at[j, m - 1], {"row": mate})

    first_tile = z * (chunks * tiles)
    for j in range(chunks):
        loads[j].wait()
        for t in range(tiles):
            tile = first_tile + j * tiles + t
            span = pl.ds(t * TI, TI)
            low = pattern[order[BPR * r], tile]
            high = pattern[order[BPR * r + 2], tile]
            gath[j][LIVE * r, :, span] = stage[j][1 - low, :, span]
            gath[j][LIVE * r + 1, :, span] = stage[j][1 + high, :, span]
        if j == 0:
            pl.semaphore_wait(barrier, 2 + (chips - 1) + (cols - 1))
        for m in range(1, chips):
            to_y(j, m, r, far(m, False)).start()
        to_core(j, r).start()

    @pl.loop(0, blocks)
    def _(q):
        slot = jnp.int32(0)
        for s in range(blocks):
            slot = jnp.where(order[s] == q, s, slot)
        inv[q] = slot

    offset = z * pairs
    occ_index = offset // NV
    vir_first = pl.multiple_of(offset - occ_index * NV, TI)
    spacing = vir[:, pl.ds(vir_first, pairs)] - occ[occ_index]
    weight[...] = 2.0 * spacing / (spacing * spacing + omega[0] * omega[0])

    for j in range(chunks):
        for m in range(1, chips):
            g = far(m, True)
            to_y(j, m, g, r ^ 1).wait_recv()
            if j < chunks - 1:
                to_x(j, m, g, x).start()
            y_core(j, m, g).start()

    for j in range(chunks):
        for m in range(1, chips):
            g = far(m, True)
            if j < chunks - 1:
                to_x(j, m, g, 1 - x).wait_recv()
                x_core(j, m, g).start()
        to_core(j, mate).wait_recv()
        for m in range(1, chips):
            g = 2 * (far(m, True) // 2) + 1 - core
            y_core(j, m, g).wait_recv()
            if j < chunks - 1:
                x_core(j, m, g).wait_recv()

        def place(q, t):
            tile = first_tile + j * tiles + t
            slot = inv[q]
            group = slot // BPR
            at = slot - BPR * group
            low = pattern[order[BPR * group], tile]
            k = jnp.where(at == 2, 1, jnp.where(at == 1, low, 0))
            return gath[j][LIVE * group + k, :, t * TI : (t + 1) * TI], pattern[q, tile].astype(jnp.float32)

        @pl.loop(0, blocks)
        def _(q):
            for t in range(tiles):
                span = pl.ds(j * wide + t * TI, TI)
                value, live = place(q, t)
                right[pl.ds(pl.multiple_of(q * BLK, BLK), BLK), span] = (
                    value.astype(jnp.float32) * (weight[:, span] * live)
                ).astype(jnp.bfloat16)

        @pl.loop(0, BPR)
        def _(i):
            for t in range(tiles):
                span = pl.ds(j * wide + t * TI, TI)
                value, live = place(BPR * r + i, t)
                left[pl.ds(pl.multiple_of(i * BLK, BLK), BLK), span] = (
                    value.astype(jnp.float32) * live
                ).astype(jnp.bfloat16)

    def share(c):
        return lax.dot_general(
            left[...],
            right[pl.ds(pl.multiple_of(c * own_cols, BLK), own_cols), :],
            (((1,), (1,)), ((), ())),
            preferred_element_type=jnp.float32,
        )

    pair = z // 2
    odd = lax.rem(pair, 2)
    inner = 2 * pair + 1 - odd
    outer = 2 * pair + odd
    relays = cols - 2

    def target(i):
        other = pair ^ (1 + i // 2)
        return 2 * other + (lax.rem(other, 2) if i % 2 == 0 else 1 - lax.rem(other, 2))

    def to_mate():
        return pltpu.make_async_remote_copy(
            src_ref=sent.at[relays], dst_ref=landed.at[0], send_sem=z_s.at[relays], recv_sem=z_r.at[0],
            device_id={"col": z ^ 1}, device_id_type=MESH,
        )

    def to_relay(i):
        return pltpu.make_async_remote_copy(
            src_ref=sent.at[i], dst_ref=relay.at[i], send_sem=z_s.at[i], recv_sem=relay_r.at[i],
            device_id={"col": z ^ 1}, device_id_type=MESH,
        )

    def to_target(i):
        m = 1 + i // 2
        return pltpu.make_async_remote_copy(
            src_ref=sent.at[i], dst_ref=landed.at[m], send_sem=z_s.at[i], recv_sem=z_r.at[m],
            device_id={"col": target(i)}, device_id_type=MESH,
        )

    gap = lax.broadcasted_iota(jnp.int32, (height, own_cols), 1) - lax.broadcasted_iota(
        jnp.int32, (height, own_cols), 0
    )

    def pack(i, value, c):
        rounded = value.astype(jnp.bfloat16)
        sent[i, pl.ds(0, height), :] = rounded
        rest = jnp.where(gap == r * height - c * own_cols, value - rounded.astype(jnp.float32), 0.0)
        sent[i, pl.ds(height, EXTRA), :] = jnp.broadcast_to(
            jnp.sum(rest, axis=0, keepdims=True), (EXTRA, own_cols)
        ).astype(jnp.bfloat16)

    def unpack(ref, i, c):
        rest = ref[i, pl.ds(height, EXTRA), :].astype(jnp.float32)[0:1]
        return ref[i, pl.ds(0, height), :].astype(jnp.float32) + jnp.where(
            gap == r * height - c * own_cols, rest, 0.0
        )

    @pl.when(z == outer)
    def _():
        for i in range(relays):
            pack(i, share(target(i)), target(i))
            to_relay(i).start()
        pack(relays, share(inner), inner)
        to_mate().start()

    @pl.when(z == inner)
    def _():
        pack(relays, share(outer), outer)
        to_mate().start()
        for i in range(relays):
            out[...] = share(target(i))
            to_relay(i).wait_recv()
            pack(i, out[...] + unpack(relay, i, target(i)), target(i))
            to_target(i).start()

    out[...] = share(z)
    for m in range(cols // 2):
        (to_mate() if m == 0 else to_target(2 * (m - 1))).wait_recv()
        out[...] += unpack(landed, m, z)
    to_mate().wait_send()
    for i in range(relays):
        to_relay(i).wait_send()
    for j in range(chunks):
        to_core(j, r).wait_send()
        for m in range(1, chips):
            g = far(m, True)
            to_y(j, m, r, far(m, False)).wait_send()
            y_core(j, m, g).wait_send()
            if j < chunks - 1:
                to_x(j, m, g, x).wait_send()
                x_core(j, m, g).wait_send()


def shards(rows, cols, b_stored, block_order, pattern, eps_occ, eps_vir, omega):
    pairs = b_stored.shape[1]
    count = pairs // TI
    tiles = 2 if count % 2 == 0 else 1
    chunks = count // tiles
    wide = tiles * TI
    chips = rows // 2
    height = b_stored.shape[0]
    own_cols = rows * height // cols
    dma = pltpu.SemaphoreType.DMA
    hop = dma((chunks, max(chips - 1, 1)))
    smem = pl.BlockSpec(memory_space=pltpu.SMEM)
    vmem = pl.BlockSpec(memory_space=pltpu.VMEM)
    return pl.pallas_call(
        functools.partial(kernel, (rows, cols, chunks, tiles)),
        out_shape=jax.ShapeDtypeStruct((height, own_cols), jnp.float32),
        in_specs=[smem, smem, smem, smem, vmem, pl.BlockSpec(memory_space=pl.ANY)],
        out_specs=vmem,
        scratch_shapes=[pltpu.VMEM((BPR, BLK, wide), jnp.bfloat16) for _ in range(chunks)]
        + [pltpu.VMEM((LIVE * rows, BLK, wide), jnp.bfloat16) for _ in range(chunks)]
        + [
            pltpu.SMEM((rows * BPR,), jnp.int32),
            pltpu.VMEM((1, pairs), jnp.float32),
            pltpu.VMEM((height, pairs), jnp.bfloat16),
            pltpu.VMEM((rows * height, pairs), jnp.bfloat16),
            pltpu.VMEM((cols - 1, height + EXTRA, own_cols), jnp.bfloat16),
            pltpu.VMEM((cols // 2, height + EXTRA, own_cols), jnp.bfloat16),
            pltpu.VMEM((cols - 2, height + EXTRA, own_cols), jnp.bfloat16),
            dma((chunks,)),
            dma((chunks,)),
            dma((chunks,)),
            hop, hop, hop, hop, hop, hop, hop, hop,
            dma((cols - 1,)),
            dma((cols // 2,)),
            dma((cols - 2,)),
        ],
        compiler_params=pltpu.CompilerParams(
            collective_id=0, has_side_effects=True, vmem_limit_bytes=56 * 2**20
        ),
        cost_estimate=pl.CostEstimate(
            flops=2 * height * rows * height * pairs, bytes_accessed=4 * height * pairs, transcendentals=0
        ),
    )(block_order, pattern, eps_occ, omega, eps_vir.reshape(1, -1), b_stored.reshape(BPR, BLK, pairs))


def solution(mesh):
    placed = (P("row", "col"), P(), P(), P(), P(), P("freq"))
    return jax.shard_map(
        functools.partial(shards, mesh.shape["row"], mesh.shape["col"]),
        mesh=mesh,
        in_specs=placed,
        out_specs=P(("freq", "row"), "col"),
        check_vma=False,
    )
```

```python
import functools
import jax
import jax.numpy as jnp
from jax import lax
from jax.experimental import pallas as pl
from jax.experimental.pallas import tpu as pltpu
from jax.sharding import PartitionSpec as P

BLK = 128
BPR = 3
LIVE = 2
NV = 3072
EXTRA = 16
TI = 256
MESH = pl.DeviceIdType.MESH


def kernel(geo, order, pattern, occ, omega, vir, b_hbm, out, *scratch):
    rows, cols, tiles = geo
    chunks = len(tiles)
    first = [sum(tiles[:j]) for j in range(chunks)]
    pairs = sum(tiles) * TI
    blocks = rows * BPR
    chips = rows // 2
    own_cols = blocks * BLK // cols
    height = BPR * BLK
    stage, gath = scratch[:chunks], scratch[chunks : 2 * chunks]
    (inv, weight, left, right, sent, landed, relay, in_sem, core_s, core_r, y_s, y_r, x_s, x_r,
     yc_s, yc_r, xc_s, xc_r, z_s, z_r, relay_r) = scratch[2 * chunks :]
    x, r, z = lax.axis_index("freq"), lax.axis_index("row"), lax.axis_index("col")
    y = r // 2
    core = r - 2 * y
    mate = 2 * y + 1 - core

    loads = [
        pltpu.make_async_copy(b_hbm.at[:, :, pl.ds(first[j] * TI, tiles[j] * TI)], stage[j], in_sem.at[j])
        for j in range(chunks)
    ]
    for load in loads:
        load.start()

    barrier = pltpu.get_barrier_semaphore()

    def greet(where):
        pl.semaphore_signal(barrier, inc=1, device_id=where, device_id_type=MESH)

    greet({"row": mate})
    greet({"freq": 1 - x})
    for m in range(1, chips):
        greet({"row": 2 * lax.rem(y + m, chips) + core})
    for m in range(1, cols):
        greet({"col": z ^ m})

    def far(m, back):
        return 2 * lax.rem(y + (chips - m if back else m), chips) + core

    def remote(ref, send, recv, where):
        return pltpu.make_async_remote_copy(
            src_ref=ref, dst_ref=ref, send_sem=send, recv_sem=recv, device_id=where, device_id_type=MESH
        )

    def part(j, g):
        return gath[j].at[pl.ds(LIVE * g, LIVE)] if j == chunks - 1 else gath[j].at[LIVE * g + x]

    def to_core(j, g):
        return remote(gath[j].at[pl.ds(LIVE * g, LIVE)], core_s.at[j], core_r.at[j], {"row": mate})

    def to_y(j, m, g, where):
        return remote(part(j, g), y_s.at[j, m - 1], y_r.at[j, m - 1], {"row": where})

    def to_x(j, m, g, half):
        return remote(gath[j].at[LIVE * g + half], x_s.at[j, m - 1], x_r.at[j, m - 1], {"freq": 1 - x})

    def y_core(j, m, g):
        return remote(part(j, g), yc_s.at[j, m - 1], yc_r.at[j, m - 1], {"row": mate})

    def x_core(j, m, g):
        return remote(gath[j].at[LIVE * g + 1 - x], xc_s.at[j, m - 1], xc_r.at[j, m - 1], {"row": mate})

    first_tile = z * sum(tiles)
    for j in range(chunks):
        loads[j].wait()
        for t in range(tiles[j]):
            tile = first_tile + first[j] + t
            span = pl.ds(t * TI, TI)
            low = pattern[order[BPR * r], tile]
            high = pattern[order[BPR * r + 2], tile]
            gath[j][LIVE * r, :, span] = stage[j][1 - low, :, span]
            gath[j][LIVE * r + 1, :, span] = stage[j][1 + high, :, span]
        if j == 0:
            pl.semaphore_wait(barrier, 2 + (chips - 1) + (cols - 1))
        for m in range(1, chips):
            to_y(j, m, r, far(m, False)).start()
        to_core(j, r).start()

    @pl.loop(0, blocks)
    def _(q):
        slot = jnp.int32(0)
        for s in range(blocks):
            slot = jnp.where(order[s] == q, s, slot)
        inv[q] = slot

    offset = z * pairs
    occ_index = offset // NV
    vir_first = pl.multiple_of(offset - occ_index * NV, TI)
    spacing = vir[:, pl.ds(vir_first, pairs)] - occ[occ_index]
    weight[...] = 2.0 * spacing / (spacing * spacing + omega[0] * omega[0])

    for j in range(chunks):
        for m in range(1, chips):
            g = far(m, True)
            to_y(j, m, g, r ^ 1).wait_recv()
            if j < chunks - 1:
                to_x(j, m, g, x).start()
            y_core(j, m, g).start()

    for j in range(chunks):
        for m in range(1, chips):
            g = far(m, True)
            if j < chunks - 1:
                to_x(j, m, g, 1 - x).wait_recv()
                x_core(j, m, g).start()
        to_core(j, mate).wait_recv()
        for m in range(1, chips):
            g = 2 * (far(m, True) // 2) + 1 - core
            y_core(j, m, g).wait_recv()
            if j < chunks - 1:
                x_core(j, m, g).wait_recv()

        def place(q, t):
            tile = first_tile + first[j] + t
            slot = inv[q]
            group = slot // BPR
            at = slot - BPR * group
            low = pattern[order[BPR * group], tile]
            k = jnp.where(at == 2, 1, jnp.where(at == 1, low, 0))
            return gath[j][LIVE * group + k, :, t * TI : (t + 1) * TI], pattern[q, tile].astype(jnp.float32)

        @pl.loop(0, blocks)
        def _(q):
            for t in range(tiles[j]):
                span = pl.ds((first[j] + t) * TI, TI)
                value, live = place(q, t)
                right[pl.ds(pl.multiple_of(q * BLK, BLK), BLK), span] = (
                    value.astype(jnp.float32) * (weight[:, span] * live)
                ).astype(jnp.bfloat16)

        @pl.loop(0, BPR)
        def _(i):
            for t in range(tiles[j]):
                span = pl.ds((first[j] + t) * TI, TI)
                value, live = place(BPR * r + i, t)
                left[pl.ds(pl.multiple_of(i * BLK, BLK), BLK), span] = (
                    value.astype(jnp.float32) * live
                ).astype(jnp.bfloat16)

    def share(c):
        return lax.dot_general(
            left[...],
            right[pl.ds(pl.multiple_of(c * own_cols, BLK), own_cols), :],
            (((1,), (1,)), ((), ())),
            preferred_element_type=jnp.float32,
        )

    pair = z // 2
    odd = lax.rem(pair, 2)
    inner = 2 * pair + 1 - odd
    outer = 2 * pair + odd
    relays = cols - 2

    def target(i):
        other = pair ^ (1 + i // 2)
        return 2 * other + (lax.rem(other, 2) if i % 2 == 0 else 1 - lax.rem(other, 2))

    def to_mate():
        return pltpu.make_async_remote_copy(
            src_ref=sent.at[relays], dst_ref=landed.at[0], send_sem=z_s.at[relays], recv_sem=z_r.at[0],
            device_id={"col": z ^ 1}, device_id_type=MESH,
        )

    def to_relay(i):
        return pltpu.make_async_remote_copy(
            src_ref=sent.at[i], dst_ref=relay.at[i], send_sem=z_s.at[i], recv_sem=relay_r.at[i],
            device_id={"col": z ^ 1}, device_id_type=MESH,
        )

    def to_target(i):
        m = 1 + i // 2
        return pltpu.make_async_remote_copy(
            src_ref=sent.at[i], dst_ref=landed.at[m], send_sem=z_s.at[i], recv_sem=z_r.at[m],
            device_id={"col": target(i)}, device_id_type=MESH,
        )

    gap = lax.broadcasted_iota(jnp.int32, (height, own_cols), 1) - lax.broadcasted_iota(
        jnp.int32, (height, own_cols), 0
    )

    def pack(i, value, c):
        rounded = value.astype(jnp.bfloat16)
        sent[i, pl.ds(0, height), :] = rounded
        rest = jnp.where(gap == r * height - c * own_cols, value - rounded.astype(jnp.float32), 0.0)
        sent[i, pl.ds(height, EXTRA), :] = jnp.broadcast_to(
            jnp.sum(rest, axis=0, keepdims=True), (EXTRA, own_cols)
        ).astype(jnp.bfloat16)

    def unpack(ref, i, c):
        rest = ref[i, pl.ds(height, EXTRA), :].astype(jnp.float32)[0:1]
        return ref[i, pl.ds(0, height), :].astype(jnp.float32) + jnp.where(
            gap == r * height - c * own_cols, rest, 0.0
        )

    @pl.when(z == outer)
    def _():
        for i in range(relays):
            pack(i, share(target(i)), target(i))
            to_relay(i).start()
        pack(relays, share(inner), inner)
        to_mate().start()

    @pl.when(z == inner)
    def _():
        pack(relays, share(outer), outer)
        to_mate().start()
        for i in range(relays):
            out[...] = share(target(i))
            to_relay(i).wait_recv()
            pack(i, out[...] + unpack(relay, i, target(i)), target(i))
            to_target(i).start()

    out[...] = share(z)
    for m in range(cols // 2):
        (to_mate() if m == 0 else to_target(2 * (m - 1))).wait_recv()
        out[...] += unpack(landed, m, z)
    to_mate().wait_send()
    for i in range(relays):
        to_relay(i).wait_send()
    for j in range(chunks):
        to_core(j, r).wait_send()
        for m in range(1, chips):
            g = far(m, True)
            to_y(j, m, r, far(m, False)).wait_send()
            y_core(j, m, g).wait_send()
            if j < chunks - 1:
                to_x(j, m, g, x).wait_send()
                x_core(j, m, g).wait_send()


def shards(rows, cols, b_stored, block_order, pattern, eps_occ, eps_vir, omega):
    pairs = b_stored.shape[1]
    count = pairs // TI
    tiles = (2,) * (count // 2 - 1) + (1, 1) if count % 2 == 0 else (1,) * count
    chunks = len(tiles)
    chips = rows // 2
    height = b_stored.shape[0]
    own_cols = rows * height // cols
    dma = pltpu.SemaphoreType.DMA
    hop = dma((chunks, max(chips - 1, 1)))
    smem = pl.BlockSpec(memory_space=pltpu.SMEM)
    vmem = pl.BlockSpec(memory_space=pltpu.VMEM)
    return pl.pallas_call(
        functools.partial(kernel, (rows, cols, tiles)),
        out_shape=jax.ShapeDtypeStruct((height, own_cols), jnp.float32),
        in_specs=[smem, smem, smem, smem, vmem, pl.BlockSpec(memory_space=pl.ANY)],
        out_specs=vmem,
        scratch_shapes=[pltpu.VMEM((BPR, BLK, n * TI), jnp.bfloat16) for n in tiles]
        + [pltpu.VMEM((LIVE * rows, BLK, n * TI), jnp.bfloat16) for n in tiles]
        + [
            pltpu.SMEM((rows * BPR,), jnp.int32),
            pltpu.VMEM((1, pairs), jnp.float32),
            pltpu.VMEM((height, pairs), jnp.bfloat16),
            pltpu.VMEM((rows * height, pairs), jnp.bfloat16),
            pltpu.VMEM((cols - 1, height + EXTRA, own_cols), jnp.bfloat16),
            pltpu.VMEM((cols // 2, height + EXTRA, own_cols), jnp.bfloat16),
            pltpu.VMEM((cols - 2, height + EXTRA, own_cols), jnp.bfloat16),
            dma((chunks,)),
            dma((chunks,)),
            dma((chunks,)),
            hop, hop, hop, hop, hop, hop, hop, hop,
            dma((cols - 1,)),
            dma((cols // 2,)),
            dma((cols - 2,)),
        ],
        compiler_params=pltpu.CompilerParams(
            collective_id=0, has_side_effects=True, vmem_limit_bytes=56 * 2**20
        ),
        cost_estimate=pl.CostEstimate(
            flops=2 * height * rows * height * pairs, bytes_accessed=4 * height * pairs, transcendentals=0
        ),
    )(block_order, pattern, eps_occ, omega, eps_vir.reshape(1, -1), b_stored.reshape(BPR, BLK, pairs))


def solution(mesh):
    placed = (P("row", "col"), P(), P(), P(), P(), P("freq"))
    return jax.shard_map(
        functools.partial(shards, mesh.shape["row"], mesh.shape["col"]),
        mesh=mesh,
        in_specs=placed,
        out_specs=P(("freq", "row"), "col"),
        check_vma=False,
    )
```

```python
import functools
import jax
import jax.numpy as jnp
from jax import lax
from jax.experimental import pallas as pl
from jax.experimental.pallas import tpu as pltpu
from jax.sharding import PartitionSpec as P

BLK = 128
BPR = 3
LIVE = 2
NV = 3072
EXTRA = 16
TI = 256
MESH = pl.DeviceIdType.MESH


def kernel(geo, order, pattern, occ, omega, vir, b_hbm, out, *scratch):
    rows, cols, tiles = geo
    chunks = len(tiles)
    first = [sum(tiles[:j]) for j in range(chunks)]
    pairs = sum(tiles) * TI
    blocks = rows * BPR
    chips = rows // 2
    own_cols = blocks * BLK // cols
    height = BPR * BLK
    stage, gath = scratch[:chunks], scratch[chunks : 2 * chunks]
    (inv, weight, left, right, sent, landed, relay, in_sem, core_s, core_r, y_s, y_r, x_s, x_r,
     yc_s, yc_r, xc_s, xc_r, z_s, z_r, relay_r) = scratch[2 * chunks :]
    x, r, z = lax.axis_index("freq"), lax.axis_index("row"), lax.axis_index("col")
    y = r // 2
    core = r - 2 * y
    mate = 2 * y + 1 - core

    loads = [
        pltpu.make_async_copy(b_hbm.at[:, :, pl.ds(first[j] * TI, tiles[j] * TI)], stage[j], in_sem.at[j])
        for j in range(chunks)
    ]
    for load in loads:
        load.start()

    barrier = pltpu.get_barrier_semaphore()

    def greet(where):
        pl.semaphore_signal(barrier, inc=1, device_id=where, device_id_type=MESH)

    greet({"row": mate})
    greet({"freq": 1 - x})
    for m in range(1, chips):
        greet({"row": 2 * lax.rem(y + m, chips) + core})
    for m in range(1, cols):
        greet({"col": z ^ m})

    def far(m, back):
        return 2 * lax.rem(y + (chips - m if back else m), chips) + core

    def remote(ref, send, recv, where):
        return pltpu.make_async_remote_copy(
            src_ref=ref, dst_ref=ref, send_sem=send, recv_sem=recv, device_id=where, device_id_type=MESH
        )

    def part(j, g):
        return gath[j].at[pl.ds(LIVE * g, LIVE)] if j == chunks - 1 else gath[j].at[LIVE * g + x]

    def to_core(j, g):
        return remote(gath[j].at[pl.ds(LIVE * g, LIVE)], core_s.at[j], core_r.at[j], {"row": mate})

    def to_y(j, m, g, where):
        return remote(part(j, g), y_s.at[j, m - 1], y_r.at[j, m - 1], {"row": where})

    def to_x(j, m, g, half):
        return remote(gath[j].at[LIVE * g + half], x_s.at[j, m - 1], x_r.at[j, m - 1], {"freq": 1 - x})

    def y_core(j, m, g):
        return remote(part(j, g), yc_s.at[j, m - 1], yc_r.at[j, m - 1], {"row": mate})

    def x_core(j, m, g):
        return remote(gath[j].at[LIVE * g + 1 - x], xc_s.at[j, m - 1], xc_r.at[j, m - 1], {"row": mate})

    first_tile = z * sum(tiles)
    for j in range(chunks):
        loads[j].wait()
        for t in range(tiles[j]):
            tile = first_tile + first[j] + t
            span = pl.ds(t * TI, TI)
            low = pattern[order[BPR * r], tile]
            high = pattern[order[BPR * r + 2], tile]
            gath[j][LIVE * r, :, span] = stage[j][1 - low, :, span]
            gath[j][LIVE * r + 1, :, span] = stage[j][1 + high, :, span]
        if j == 0:
            pl.semaphore_wait(barrier, 2 + (chips - 1) + (cols - 1))
        for m in range(1, chips):
            to_y(j, m, r, far(m, False)).start()
        to_core(j, r).start()

    @pl.loop(0, blocks)
    def _(q):
        slot = jnp.int32(0)
        for s in range(blocks):
            slot = jnp.where(order[s] == q, s, slot)
        inv[q] = slot

    offset = z * pairs
    occ_index = offset // NV
    vir_first = pl.multiple_of(offset - occ_index * NV, TI)
    spacing = vir[:, pl.ds(vir_first, pairs)] - occ[occ_index]
    weight[...] = 2.0 * spacing / (spacing * spacing + omega[0] * omega[0])

    for j in range(chunks):
        for m in range(1, chips):
            g = far(m, True)
            to_y(j, m, g, r ^ 1).wait_recv()
            if j < chunks - 1:
                to_x(j, m, g, x).start()
            y_core(j, m, g).start()

    for j in range(chunks):
        for m in range(1, chips):
            g = far(m, True)
            if j < chunks - 1:
                to_x(j, m, g, 1 - x).wait_recv()
                x_core(j, m, g).start()
        to_core(j, mate).wait_recv()
        for m in range(1, chips):
            g = 2 * (far(m, True) // 2) + 1 - core
            y_core(j, m, g).wait_recv()
            if j < chunks - 1:
                x_core(j, m, g).wait_recv()

        def place(q, t):
            tile = first_tile + first[j] + t
            slot = inv[q]
            group = slot // BPR
            at = slot - BPR * group
            low = pattern[order[BPR * group], tile]
            k = jnp.where(at == 2, 1, jnp.where(at == 1, low, 0))
            return gath[j][LIVE * group + k, :, t * TI : (t + 1) * TI], pattern[q, tile].astype(jnp.float32)

        @pl.loop(0, blocks)
        def _(q):
            for t in range(tiles[j]):
                span = pl.ds((first[j] + t) * TI, TI)
                value, live = place(q, t)
                right[pl.ds(pl.multiple_of(q * BLK, BLK), BLK), span] = (
                    value.astype(jnp.float32) * (weight[:, span] * live)
                ).astype(jnp.bfloat16)

        @pl.loop(0, BPR)
        def _(i):
            for t in range(tiles[j]):
                span = pl.ds((first[j] + t) * TI, TI)
                value, live = place(BPR * r + i, t)
                left[pl.ds(pl.multiple_of(i * BLK, BLK), BLK), span] = (
                    value.astype(jnp.float32) * live
                ).astype(jnp.bfloat16)

    def share(c):
        return lax.dot_general(
            left[...],
            right[pl.ds(pl.multiple_of(c * own_cols, BLK), own_cols), :],
            (((1,), (1,)), ((), ())),
            preferred_element_type=jnp.float32,
        )

    pair = z // 2
    odd = lax.rem(pair, 2)
    inner = 2 * pair + 1 - odd
    outer = 2 * pair + odd
    relays = cols - 2

    def target(i):
        other = pair ^ (1 + i // 2)
        return 2 * other + (lax.rem(other, 2) if i % 2 == 0 else 1 - lax.rem(other, 2))

    def to_mate():
        return pltpu.make_async_remote_copy(
            src_ref=sent.at[relays], dst_ref=landed.at[0], send_sem=z_s.at[relays], recv_sem=z_r.at[0],
            device_id={"col": z ^ 1}, device_id_type=MESH,
        )

    def to_relay(i):
        return pltpu.make_async_remote_copy(
            src_ref=sent.at[i], dst_ref=relay.at[i], send_sem=z_s.at[i], recv_sem=relay_r.at[i],
            device_id={"col": z ^ 1}, device_id_type=MESH,
        )

    def to_target(i):
        m = 1 + i // 2
        return pltpu.make_async_remote_copy(
            src_ref=sent.at[i], dst_ref=landed.at[m], send_sem=z_s.at[i], recv_sem=z_r.at[m],
            device_id={"col": target(i)}, device_id_type=MESH,
        )

    gap = lax.broadcasted_iota(jnp.int32, (height, own_cols), 1) - lax.broadcasted_iota(
        jnp.int32, (height, own_cols), 0
    )

    def pack(i, value, c):
        rounded = value.astype(jnp.bfloat16)
        sent[i, pl.ds(0, height), :] = rounded
        rest = jnp.where(gap == r * height - c * own_cols, value - rounded.astype(jnp.float32), 0.0)
        sent[i, pl.ds(height, EXTRA), :] = jnp.broadcast_to(
            jnp.sum(rest, axis=0, keepdims=True), (EXTRA, own_cols)
        ).astype(jnp.bfloat16)

    def unpack(ref, i, c):
        rest = ref[i, pl.ds(height, EXTRA), :].astype(jnp.float32)[0:1]
        return ref[i, pl.ds(0, height), :].astype(jnp.float32) + jnp.where(
            gap == r * height - c * own_cols, rest, 0.0
        )

    @pl.when(z == outer)
    def _():
        for i in range(relays):
            pack(i, share(target(i)), target(i))
            to_relay(i).start()
        pack(relays, share(inner), inner)
        to_mate().start()

    @pl.when(z == inner)
    def _():
        pack(relays, share(outer), outer)
        to_mate().start()
        for i in range(relays):
            out[...] = share(target(i))
            to_relay(i).wait_recv()
            pack(i, out[...] + unpack(relay, i, target(i)), target(i))
            to_target(i).start()

    out[...] = share(z)
    for m in range(cols // 2):
        (to_mate() if m == 0 else to_target(2 * (m - 1))).wait_recv()
        out[...] += unpack(landed, m, z)
    to_mate().wait_send()
    for i in range(relays):
        to_relay(i).wait_send()
    for j in range(chunks):
        to_core(j, r).wait_send()
        for m in range(1, chips):
            g = far(m, True)
            to_y(j, m, r, far(m, False)).wait_send()
            y_core(j, m, g).wait_send()
            if j < chunks - 1:
                to_x(j, m, g, x).wait_send()
                x_core(j, m, g).wait_send()


def shards(rows, cols, b_stored, block_order, pattern, eps_occ, eps_vir, omega):
    pairs = b_stored.shape[1]
    count = pairs // TI
    tiles = (count // 2, count // 2 - 1, 1) if count % 2 == 0 and count > 2 else (1,) * count
    chunks = len(tiles)
    chips = rows // 2
    height = b_stored.shape[0]
    own_cols = rows * height // cols
    dma = pltpu.SemaphoreType.DMA
    hop = dma((chunks, max(chips - 1, 1)))
    smem = pl.BlockSpec(memory_space=pltpu.SMEM)
    vmem = pl.BlockSpec(memory_space=pltpu.VMEM)
    return pl.pallas_call(
        functools.partial(kernel, (rows, cols, tiles)),
        out_shape=jax.ShapeDtypeStruct((height, own_cols), jnp.float32),
        in_specs=[smem, smem, smem, smem, vmem, pl.BlockSpec(memory_space=pl.ANY)],
        out_specs=vmem,
        scratch_shapes=[pltpu.VMEM((BPR, BLK, n * TI), jnp.bfloat16) for n in tiles]
        + [pltpu.VMEM((LIVE * rows, BLK, n * TI), jnp.bfloat16) for n in tiles]
        + [
            pltpu.SMEM((rows * BPR,), jnp.int32),
            pltpu.VMEM((1, pairs), jnp.float32),
            pltpu.VMEM((height, pairs), jnp.bfloat16),
            pltpu.VMEM((rows * height, pairs), jnp.bfloat16),
            pltpu.VMEM((cols - 1, height + EXTRA, own_cols), jnp.bfloat16),
            pltpu.VMEM((cols // 2, height + EXTRA, own_cols), jnp.bfloat16),
            pltpu.VMEM((cols - 2, height + EXTRA, own_cols), jnp.bfloat16),
            dma((chunks,)),
            dma((chunks,)),
            dma((chunks,)),
            hop, hop, hop, hop, hop, hop, hop, hop,
            dma((cols - 1,)),
            dma((cols // 2,)),
            dma((cols - 2,)),
        ],
        compiler_params=pltpu.CompilerParams(
            collective_id=0, has_side_effects=True, vmem_limit_bytes=56 * 2**20
        ),
        cost_estimate=pl.CostEstimate(
            flops=2 * height * rows * height * pairs, bytes_accessed=4 * height * pairs, transcendentals=0
        ),
    )(block_order, pattern, eps_occ, omega, eps_vir.reshape(1, -1), b_stored.reshape(BPR, BLK, pairs))


def solution(mesh):
    placed = (P("row", "col"), P(), P(), P(), P(), P("freq"))
    return jax.shard_map(
        functools.partial(shards, mesh.shape["row"], mesh.shape["col"]),
        mesh=mesh,
        in_specs=placed,
        out_specs=P(("freq", "row"), "col"),
        check_vma=False,
    )
```
